32 devices in a mesh: groups: 2 (over y), leaf: 4 (over z), rhs: 2 (over x), half: 2 (over core).
Axes of the slice: x: 2, y: 2, z: 4, core: 2. Of those that a mesh axis runs over, the one named last changes fastest.
Arguments:
- sources: bfloat16 [2, 32, 16384], P(None, 'rhs', ('groups', 'leaf', 'half')), parts along dimension 2, may hold values from -6 to 6
- probe_field: bfloat16 [2, 32, 16384], P(None, 'rhs', ('groups', 'leaf', 'half')), parts along dimension 2, may hold values from -6 to 6
- factor_weight: bfloat16 [6, 128, 2, 2, 128, 128], P(None, ('groups', 'leaf', 'half')), parts along dimension 1, may hold values from -0.25 to 0.25
- factor_pattern: int32 [6, 128, 2], P(None, ('groups', 'leaf', 'half')), parts along dimension 1, may hold values from 0 to 15, as said below
- near_weight: bfloat16 [128, 2, 2, 128, 128], P(('groups', 'leaf', 'half'), 'rhs'), parts along dimension 0, may hold values from -0.25 to 0.25
- near_index: int32 [128, 2], P(('groups', 'leaf', 'half')), parts along dimension 0, may hold values from 0 to 7
- tree_order: int32 [16384], P(('groups', 'leaf', 'half')), parts along dimension 0, may hold values from 0 to 1023, as said below
Outputs:
- forward_field: bfloat16 [2, 32, 16384], P(None, 'rhs', ('groups', 'leaf', 'half')), parts along dimension 2
- adjoint_field: bfloat16 [2, 32, 16384], P(None, 'rhs', ('groups', 'leaf', 'half')), parts along dimension 2
The draws below stay inside these ranges and needn't reach their ends.
There are 2 independent parts, one for each index of `groups`. The reference program is written for one: setup_inputs(seed, part) draws one part's arguments, and reference() takes and returns one part's arrays. A program takes and returns all parts, laid end to end along the dimension named above; each array names one. Nothing has to cross between parts.
Inputs may be any that keep to these rules, and one draw needn't show every extreme that they name: `factor_pattern`: at levels below 3 every entry is below 8 (a block of the same cluster); at higher levels an entry below 8 names a block of the same cluster and an entry p of 8 or more names block p - 8 of the partner cluster. `tree_order`: each aligned run of 1024 entries (one cluster) is a permutation of 0 to 1023.
All inputs are finite; a program needn't handle non-finite values.
Results may differ from the reference program's by a relative error of at most 0.017.
Values may be sent and summed in bfloat16 or wider, within the bound.
A program may use at most 64 MiB of HBM per device.

```python
import jax
import jax.numpy as jnp
from jax import lax

BLK = 128
NB = 8
NRHS = 32
K = 2
LOC = 3
CLUSTERS = 8
LEVELS = 6
NEAR = 2
BLOCKS = 64
ROWS = 8192


def draw_factor_pattern(key, part):
    key = jax.random.fold_in(key, 7)
    drawn = jax.random.randint(key, (LEVELS, BLOCKS, K), 0, 2 * NB, dtype=jnp.int32)
    level_ids = jnp.arange(LEVELS, dtype=jnp.int32)[:, None, None]
    picked = jnp.where(level_ids < LOC, drawn % NB, drawn)
    picked = picked.at[LEVELS - 1, 0, 0].set(2 * NB - 1)
    return picked.at[0, 0, 1].set(0)


def shuffle_one(subkey):
    return jax.random.permutation(subkey, NB * BLK)


def draw_tree_order(key, part):
    key = jax.random.fold_in(key, 13)
    subkeys = jax.random.split(key, CLUSTERS)
    shuffles = jax.vmap(shuffle_one)(subkeys)
    return shuffles.reshape(-1).astype(jnp.int32)


def with_ends(entries, rng, low, largest):
    longest = entries.shape.index(max(entries.shape))
    spots = []
    for shift in (0, 1):
        where = [jax.random.randint(jax.random.fold_in(rng, axis), (), 0, length) for axis, length in enumerate(entries.shape)]
        where[longest] = (where[longest] + shift) % entries.shape[longest]
        spots.append(tuple(where))
    return entries.at[spots[0]].set(low).at[spots[1]].set(largest)


def block_levels(key, shape, pieces, low, top_value):
    factor_of = 1.0
    for dim, blocks in pieces:
        steps = jax.random.uniform(jax.random.fold_in(jax.random.fold_in(key, 6), dim), (blocks,), jnp.float32, low / len(pieces), top_value / len(pieces))
        factor_of = factor_of * jnp.repeat(jnp.exp(steps), shape[dim] // blocks).reshape((-1,) + (1,) * (len(shape) - 1 - dim))
    return factor_of


def normal_values(key, dims, width, bound, cuts=(), kind=jnp.bfloat16):
    gain = block_levels(key, dims, cuts, -0.22, 0.18) if cuts else 1.0
    values = jax.random.normal(key, dims, jnp.float32) * width * gain
    return jnp.minimum(jnp.maximum(values, -bound), bound).astype(kind)


def setup_inputs(seed: int = 0, part: int = 0) -> dict:
    key_list = jax.random.split(jax.random.key(seed), 8)
    part_keys = jax.random.split(jax.random.fold_in(key_list[7], part), 8)
    return {
        "sources": normal_values(part_keys[0], (2, NRHS, ROWS), 1.0, 6.0, ((1, 2), (2, 8))),
        "probe_field": normal_values(part_keys[1], (2, NRHS, ROWS), 1.0, 6.0, ((1, 2), (2, 8))),
        "factor_weight": normal_values(part_keys[2], (LEVELS, BLOCKS, K, 2, BLK, BLK), (2 * K * BLK) ** -0.5, 0.25, ((1, 8),)),
        "factor_pattern": draw_factor_pattern(jax.random.fold_in(jax.random.fold_in(key_list[7], part), 71), part),
        "near_weight": normal_values(part_keys[4], (BLOCKS, NEAR, 2, BLK, BLK), (2 * NEAR * BLK) ** -0.5, 0.25, ((0, 8), (1, 2))),
        "near_index": with_ends(jax.random.randint(part_keys[5], (BLOCKS, NEAR), 0, NB), jax.random.fold_in(part_keys[5], 1), 0, NB - 1).astype(jnp.int32),
        "tree_order": draw_tree_order(jax.random.fold_in(jax.random.fold_in(key_list[7], part), 71), part),
    }


def into_tree(field_values, tree_order):
    cluster_rows = NB * BLK
    total_rows = field_values.shape[2]
    gathered_rows = (jnp.arange(total_rows, dtype=jnp.int32) // cluster_rows) * cluster_rows + tree_order.astype(jnp.int32)
    return field_values[:, :, gathered_rows], gathered_rows


def blocked(field_values):
    return field_values.reshape(2, field_values.shape[1], field_values.shape[2] // BLK, BLK)


def level_targets(pattern, level_id):
    pattern = pattern.astype(jnp.int32)
    block_ids = jnp.arange(pattern.shape[0], dtype=jnp.int32)[:, None]
    cluster = block_ids // NB
    if level_id < LOC:
        return cluster * NB + pattern
    flipped = jnp.bitwise_xor(cluster, jnp.int32(1 << (level_id - LOC)))
    return jnp.where(pattern >= NB, flipped * NB + pattern - NB, cluster * NB + pattern)


def apply_global(current, weights, targets):
    chosen = current[:, :, targets, :].astype(jnp.float32)
    matrix = weights.astype(jnp.float32)
    highest = lax.Precision.HIGHEST

    def product(left_part, right_part):
        return jnp.einsum('cgkr,gksr->cgs', left_part, right_part, precision=highest)

    real_part = product(chosen[0], matrix[:, :, 0]) - product(chosen[1], matrix[:, :, 1])
    imag_part = product(chosen[1], matrix[:, :, 0]) + product(chosen[0], matrix[:, :, 1])
    return jnp.stack([real_part, imag_part])


def spread_global(current, weights, targets):
    values = current.astype(jnp.float32)
    matrix = weights.astype(jnp.float32)
    highest = lax.Precision.HIGHEST

    def product(left_part, right_part):
        return jnp.einsum('cgs,gksr->cgkr', left_part, right_part, precision=highest)

    real_part = product(values[0], matrix[:, :, 0]) + product(values[1], matrix[:, :, 1])
    imag_part = product(values[1], matrix[:, :, 0]) - product(values[0], matrix[:, :, 1])
    contrib = jnp.stack([real_part, imag_part])
    summed = jnp.zeros(current.shape, jnp.float32)
    return summed.at[:, :, targets].add(contrib)


def reference(sources, probe_field, factor_weight, factor_pattern, near_weight, near_index, tree_order):
    x_tree, gathered_rows = into_tree(sources, tree_order)
    v_tree, unused_rows = into_tree(probe_field, tree_order)
    levels = factor_weight.shape[0]
    block_ids = jnp.arange(near_index.shape[0], dtype=jnp.int32)[:, None]
    near_targets = (block_ids // NB) * NB + near_index.astype(jnp.int32)

    current = blocked(x_tree)
    for level_id in range(levels):
        targets = level_targets(factor_pattern[level_id], level_id)
        current = apply_global(current, factor_weight[level_id], targets).astype(jnp.bfloat16)
    near_forward = apply_global(blocked(x_tree), near_weight, near_targets)
    forward_tree = (current.astype(jnp.float32) + near_forward).astype(jnp.bfloat16).reshape(sources.shape)

    current = blocked(v_tree)
    for level_id in reversed(range(levels)):
        targets = level_targets(factor_pattern[level_id], level_id)
        current = spread_global(current, factor_weight[level_id], targets).astype(jnp.bfloat16)
    near_adjoint = spread_global(blocked(v_tree), near_weight, near_targets)
    adjoint_tree = (current.astype(jnp.float32) + near_adjoint).astype(jnp.bfloat16).reshape(sources.shape)

    forward_field = jnp.zeros_like(sources).at[:, :, gathered_rows].set(forward_tree)
    adjoint_field = jnp.zeros_like(sources).at[:, :, gathered_rows].set(adjoint_tree)
    return forward_field, adjoint_field
```

```python
import functools

import jax
import jax.numpy as jnp
from jax import lax
from jax.experimental import pallas as pl
from jax.experimental.pallas import tpu as pltpu
from jax.sharding import PartitionSpec as P

BLK = 128
LOC = 3
BF = jnp.bfloat16
F32 = jnp.float32
MESH = pl.DeviceIdType.MESH


def flip(value, bit):
    return value + (1 - 2 * ((value // bit) % 2)) * bit


def partner_of(t):
    if t == 0:
        return {"half": flip(lax.axis_index("half"), 1)}
    return {"leaf": flip(lax.axis_index("leaf"), 2 ** (t - 1))}


def dot_nn(a, b):
    return lax.dot_general(a, b, (((1,), (0,)), ((), ())), preferred_element_type=F32)


def dot_nt(a, b):
    return lax.dot_general(a, b, (((1,), (1,)), ((), ())), preferred_element_type=F32)


def combine_forward(out, cols):
    real = out[:cols, :BLK] - out[cols:, BLK:]
    imag = out[cols:, :BLK] + out[:cols, BLK:]
    return jnp.concatenate([real, imag], axis=0)


def conj_rows(value, cols):
    real, imag = value[:cols], value[cols:]
    return jnp.concatenate(
        [jnp.concatenate([real, imag], axis=1), jnp.concatenate([imag, -real], axis=1)], axis=0
    )


def kernel(
    levels, nb, cols, near, n_rhs,
    src, prb, fw, pat, nw, nidx, order,
    out_f, out_a,
    wv, nwv, raw, perm, xt, vt, fl, fx, ff, bcur, contrib, aown, asend, arecv,
    nf, na, nsend, nret,
    wsem, nwsem, rawsem, xs_sem, xr_sem, fs_sem, fr_sem, as_sem, ar_sem, ns_sem, nr_sem,
):
    rows = nb * BLK
    height = 2 * cols
    tops = levels - LOC
    me_rhs = lax.axis_index("rhs")

    def peer(d):
        return {"rhs": lax.rem(me_rhs + d, n_rhs)}

    def origin(d):
        return {"rhs": lax.rem(me_rhs + n_rhs - d, n_rhs)}

    barrier = pltpu.get_barrier_semaphore()
    for t in range(tops):
        pl.semaphore_signal(barrier, inc=1, device_id=partner_of(t), device_id_type=MESH)
    for d in range(1, n_rhs):
        pl.semaphore_signal(barrier, inc=1, device_id=peer(d), device_id_type=MESH)

    raw_copies = [
        pltpu.make_async_copy(src, raw.at[0, 0], rawsem.at[0]),
        pltpu.make_async_copy(prb, raw.at[0, 1], rawsem.at[1]),
    ]
    for copy in raw_copies:
        copy.start()
    wcopies = [pltpu.make_async_copy(fw.at[l], wv.at[l], wsem.at[l]) for l in range(levels)]
    order_of_levels = []
    for l in range((levels + 1) // 2):
        for pick in (levels - 1 - l, l):
            if pick not in order_of_levels:
                order_of_levels.append(pick)
    for l in order_of_levels:
        wcopies[l].start()
    ncopy = pltpu.make_async_copy(nw, nwv, nwsem)
    ncopy.start()
    wready = set()

    def ready(l):
        if l not in wready:
            wcopies[l].wait()
            wready.add(l)

    pl.semaphore_wait(barrier, tops + n_rhs - 1)
    raw_sends = []
    for d in range(1, n_rhs):
        for which, ref in ((0, src), (1, prb)):
            copy = pltpu.make_async_remote_copy(
                src_ref=ref,
                dst_ref=raw.at[d, which],
                send_sem=xs_sem.at[d - 1, which],
                recv_sem=xr_sem.at[d - 1, which],
                device_id=peer(d),
                device_id_type=MESH,
            )
            copy.start()
            raw_sends.append(copy)

    wanted = [jnp.broadcast_to(order[q : q + 1, :], (16, BLK)) for q in range(nb)]
    step_iota = lax.broadcasted_iota(jnp.int32, (16, BLK), 0)

    def build(j, carry):
        base = pl.multiple_of(j * 16, 16)
        line = step_iota + base
        for q in range(nb):
            perm[pl.ds(base, 16), q * BLK : (q + 1) * BLK] = jnp.where(
                wanted[q] == line, 1.0, 0.0
            ).astype(BF)
        return carry

    lax.fori_loop(0, rows // 16, build, 0, unroll=4)

    def to_tree(d):
        stacked = jnp.concatenate(
            [raw[d, 0, 0], raw[d, 0, 1], raw[d, 1, 0], raw[d, 1, 1]], axis=0
        )
        for n in range(nb // 2):
            lo = n * 2 * BLK
            got = dot_nn(stacked, perm[:, lo : lo + 2 * BLK]).astype(BF)
            for e in range(2):
                xt[d, 2 * n + e] = got[:height, e * BLK : (e + 1) * BLK]
                vt[d, 2 * n + e] = got[height:, e * BLK : (e + 1) * BLK]

    def big(l, g):
        return jnp.concatenate(
            [wv[l, g, 0].reshape(2 * BLK, BLK), wv[l, g, 1].reshape(2 * BLK, BLK)], axis=1
        )

    def forward_level(l, cur, dst):
        ready(l)
        for g in range(nb):
            lhs = jnp.concatenate(
                [cur[pat[l, 0, g]], cur[pat[l, 1, g]]], axis=1
            )
            dst[g] = combine_forward(dot_nt(lhs, big(l, g)), cols).astype(BF)

    def masked_sum(pieces, spots, h):
        total = jnp.where(spots[0] == h, pieces[0], 0.0)
        for spot, piece in zip(spots[1:], pieces[1:]):
            total = total + jnp.where(spot == h, piece, 0.0)
        return total

    def adjoint_level(l, cur, dst):
        ready(l)
        for g in range(nb):
            out = dot_nn(conj_rows(cur[g], cols), big(l, g))
            contrib[2 * g] = out[:, :BLK]
            contrib[2 * g + 1] = out[:, BLK:]
        spots = [jnp.full((height, BLK), pat[l, j % 2, j // 2], jnp.int32) for j in range(2 * nb)]

        def sum_for(h):
            return masked_sum([contrib[j] for j in range(2 * nb)], spots, h)

        if l < LOC:

            def local(h, carry):
                dst[h] = sum_for(h).astype(BF)
                return carry

            lax.fori_loop(0, nb, local, 0)
            return None
        t = l - LOC

        def far(h, carry):
            asend[t, h] = sum_for(h + nb).astype(BF)
            return carry

        lax.fori_loop(0, nb, far, 0)
        copy = pltpu.make_async_remote_copy(
            src_ref=asend.at[t],
            dst_ref=arecv.at[t],
            send_sem=as_sem.at[t],
            recv_sem=ar_sem.at[t],
            device_id=partner_of(t),
            device_id_type=MESH,
        )
        copy.start()

        def own(h, carry):
            aown[h] = sum_for(h)
            return carry

        lax.fori_loop(0, nb, own, 0)
        return copy

    def adjoint_arrive(l, copy):
        copy.wait_recv()
        t = l - LOC
        for h in range(nb):
            bcur[l, h] = (aown[h] + arecv[t, h].astype(F32)).astype(BF)

    def forward_send(t):
        copy = pltpu.make_async_remote_copy(
            src_ref=fx[t].at[pl.ds(0, nb)],
            dst_ref=fx[t].at[pl.ds(nb, nb)],
            send_sem=fs_sem.at[t],
            recv_sem=fr_sem.at[t],
            device_id=partner_of(t),
            device_id_type=MESH,
        )
        copy.start()
        return copy

    def near_parts(d):
        m0 = me_rhs * near
        for g in range(nb):
            acc = None
            for m in range(near):
                got = dot_nt(xt[d, nidx[m0 + m, g]], nwv[g, m].reshape(2 * BLK, BLK))
                got = combine_forward(got, cols)
                acc = got if acc is None else acc + got
            if d == 0:
                nf[g] = acc
            else:
                nsend[d - 1, 0, g] = acc.astype(BF)
        for h in range(nb):
            na[h] = jnp.zeros((height, BLK), F32) if d == 0 else na[h]
        for m in range(near):
            for g in range(nb):
                contrib[g] = dot_nn(
                    conj_rows(vt[d, g], cols), nwv[g, m].reshape(2 * BLK, BLK)
                )
            spots = [jnp.full((height, BLK), nidx[m0 + m, g], jnp.int32) for g in range(nb)]

            def one(h, carry):
                total = masked_sum([contrib[g] for g in range(nb)], spots, h)
                if d == 0:
                    na[h] = na[h] + total
                elif near == 1:
                    nsend[d - 1, 1, h] = total.astype(BF)
                else:
                    before = nsend[d - 1, 1, h].astype(F32) if m else 0.0
                    nsend[d - 1, 1, h] = (before + total).astype(BF)
                return carry

            lax.fori_loop(0, nb, one, 0)

    for copy in raw_copies:
        copy.wait()
    to_tree(0)
    sends_a = {}
    sends_f = {}
    sends_a[levels - 1] = adjoint_level(levels - 1, vt.at[0], None)
    cur = xt.at[0]
    for l in range(LOC):
        dst = fx[0].at[pl.ds(0, nb)] if l == LOC - 1 else fl.at[l]
        forward_level(l, cur, dst)
        cur = dst
    sends_f[0] = forward_send(0)

    ncopy.wait()
    near_parts(0)
    near_sends = []
    for d in range(1, n_rhs):
        raw_sends[2 * (d - 1)].wait_recv()
        raw_sends[2 * (d - 1) + 1].wait_recv()
        to_tree(d)
        near_parts(d)
        copy = pltpu.make_async_remote_copy(
            src_ref=nsend.at[d - 1],
            dst_ref=nret.at[d - 1],
            send_sem=ns_sem.at[d - 1],
            recv_sem=nr_sem.at[d - 1],
            device_id=origin(d),
            device_id_type=MESH,
        )
        copy.start()
        near_sends.append(copy)

    for i in range(tops):
        sends_f[i].wait_recv()
        last = i == tops - 1
        forward_level(LOC + i, fx[i], ff if last else fx[i + 1].at[pl.ds(0, nb)])
        if not last:
            sends_f[i + 1] = forward_send(i + 1)
        la = levels - 1 - i
        adjoint_arrive(la, sends_a[la])
        if not last:
            sends_a[la - 1] = adjoint_level(la - 1, bcur.at[la], None)
    for l in reversed(range(LOC)):
        adjoint_level(l, bcur.at[l + 1], bcur.at[l])

    for copy in near_sends:
        copy.wait_recv()
    lines_f, lines_a = [], []
    for g in range(nb):
        tf, ta = nf[g], na[g]
        for d in range(1, n_rhs):
            tf = tf + nret[d - 1, 0, g].astype(F32)
            ta = ta + nret[d - 1, 1, g].astype(F32)
        lines_f.append((ff[g].astype(F32) + tf).astype(BF))
        lines_a.append((bcur[0, g].astype(F32) + ta).astype(BF))
    tree = jnp.concatenate(
        [jnp.concatenate(lines_f, axis=1), jnp.concatenate(lines_a, axis=1)], axis=0
    )
    for n in range(nb // 2):
        lo = n * 2 * BLK
        got = dot_nt(tree, perm[lo : lo + 2 * BLK, :]).astype(BF)
        for z in range(2):
            out_f[z, :, lo : lo + 2 * BLK] = got[z * cols : (z + 1) * cols]
            out_a[z, :, lo : lo + 2 * BLK] = got[height + z * cols : height + (z + 1) * cols]

    for copy in raw_sends + near_sends + list(sends_f.values()) + list(sends_a.values()):
        copy.wait_send()


def body(n_rhs, sources, probe_field, factor_weight, factor_pattern, near_weight, near_index, tree_order):
    columns = sources.shape[1]
    rows = sources.shape[2]
    cols = -(-columns // 16) * 16
    if cols != columns:
        widen = ((0, 0), (0, cols - columns), (0, 0))
        sources = jnp.pad(sources, widen)
        probe_field = jnp.pad(probe_field, widen)
    nb = rows // BLK
    levels = factor_weight.shape[0]
    tops = levels - LOC
    near = near_weight.shape[1]
    height = 2 * cols
    block = (height, BLK)
    others = n_rhs - 1
    dma = pltpu.SemaphoreType.DMA
    any_spec = pl.BlockSpec(memory_space=pltpu.HBM)
    smem = pl.BlockSpec(memory_space=pltpu.SMEM)
    vmem = pl.BlockSpec(memory_space=pltpu.VMEM)
    out = jax.ShapeDtypeStruct((2, cols, rows), BF)
    forward_field, adjoint_field = pl.pallas_call(
        functools.partial(kernel, levels, nb, cols, near, n_rhs),
        out_shape=(out, out),
        in_specs=[any_spec, any_spec, any_spec, smem, any_spec, smem, vmem],
        out_specs=(vmem, vmem),
        scratch_shapes=[
            pltpu.VMEM(factor_weight.shape, BF),
            pltpu.VMEM(near_weight.shape, BF),
            pltpu.VMEM((n_rhs, 2, 2, cols, rows), BF),
            pltpu.VMEM((rows, rows), BF),
            pltpu.VMEM((n_rhs, nb) + block, BF),
            pltpu.VMEM((n_rhs, nb) + block, BF),
            pltpu.VMEM((LOC, nb) + block, BF),
            [pltpu.VMEM((2 * nb,) + block, BF) for _ in range(tops)],
            pltpu.VMEM((nb,) + block, BF),
            pltpu.VMEM((levels, nb) + block, BF),
            pltpu.VMEM((2 * nb,) + block, F32),
            pltpu.VMEM((nb,) + block, F32),
            pltpu.VMEM((tops, nb) + block, BF),
            pltpu.VMEM((tops, nb) + block, BF),
            pltpu.VMEM((nb,) + block, F32),
            pltpu.VMEM((nb,) + block, F32),
            pltpu.VMEM((others, 2, nb) + block, BF),
            pltpu.VMEM((others, 2, nb) + block, BF),
            dma((levels,)),
            dma,
            dma((2,)),
            dma((others, 2)),
            dma((others, 2)),
            dma((tops,)),
            dma((tops,)),
            dma((tops,)),
            dma((tops,)),
            dma((others,)),
            dma((others,)),
        ],
        compiler_params=pltpu.CompilerParams(
            collective_id=0, has_side_effects=True, vmem_limit_bytes=60 * 2**20
        ),
    )(
        sources,
        probe_field,
        factor_weight,
        jnp.swapaxes(factor_pattern, 1, 2),
        near_weight,
        jnp.swapaxes(near_index, 0, 1),
        tree_order.reshape(nb, BLK),
    )
    return forward_field[:, :columns], adjoint_field[:, :columns]


def solution(mesh):
    rows = ("groups", "leaf", "half")
    return jax.shard_map(
        functools.partial(body, mesh.shape["rhs"]),
        mesh=mesh,
        in_specs=(
            P(None, "rhs", rows),
            P(None, "rhs", rows),
            P(None, rows, None, None, None, None),
            P(None, rows, None),
            P(rows, "rhs", None, None, None),
            P(rows, None),
            P(rows),
        ),
        out_specs=(P(None, "rhs", rows), P(None, "rhs", rows)),
        check_vma=False,
    )
```

```python
import functools

import jax
import jax.numpy as jnp
from jax import lax
from jax.experimental import pallas as pl
from jax.experimental.pallas import tpu as pltpu
from jax.sharding import PartitionSpec as P

BLK = 128
LOC = 3
BF = jnp.bfloat16
F32 = jnp.float32
MESH = pl.DeviceIdType.MESH


def flip(value, bit):
    return value + (1 - 2 * ((value // bit) % 2)) * bit


def partner_of(t):
    if t == 0:
        return {"half": flip(lax.axis_index("half"), 1)}
    return {"leaf": flip(lax.axis_index("leaf"), 2 ** (t - 1))}


def dot_nn(a, b):
    return lax.dot_general(a, b, (((1,), (0,)), ((), ())), preferred_element_type=F32)


def dot_nt(a, b):
    return lax.dot_general(a, b, (((1,), (1,)), ((), ())), preferred_element_type=F32)


def combine_forward(out, cols):
    real = out[:cols, :BLK] - out[cols:, BLK:]
    imag = out[cols:, :BLK] + out[:cols, BLK:]
    return jnp.concatenate([real, imag], axis=0)


def conj_rows(value, cols):
    real, imag = value[:cols], value[cols:]
    return jnp.concatenate(
        [jnp.concatenate([real, imag], axis=1), jnp.concatenate([imag, -real], axis=1)], axis=0
    )


def kernel(
    levels, nb, cols, near, n_rhs,
    src, prb, fw, pat, nw, nidx, order,
    out,
    wv, nwv, raw, perm, xt, vt, fl, fx, ff, bcur, contrib, aown, asend, arecv,
    nf, na, nsend, nret,
    wsem, nwsem, rawsem, xs_sem, xr_sem, fs_sem, fr_sem, as_sem, ar_sem, ns_sem, nr_sem,
):
    rows = nb * BLK
    height = 2 * cols
    tops = levels - LOC
    me_rhs = lax.axis_index("rhs")

    def peer(d):
        return {"rhs": lax.rem(me_rhs + d, n_rhs)}

    def origin(d):
        return {"rhs": lax.rem(me_rhs + n_rhs - d, n_rhs)}

    barrier = pltpu.get_barrier_semaphore()
    for t in range(tops):
        pl.semaphore_signal(barrier, inc=1, device_id=partner_of(t), device_id_type=MESH)
    for d in range(1, n_rhs):
        pl.semaphore_signal(barrier, inc=1, device_id=peer(d), device_id_type=MESH)

    raw_copies = [
        pltpu.make_async_copy(src, raw.at[0, 0], rawsem.at[0]),
        pltpu.make_async_copy(prb, raw.at[0, 1], rawsem.at[1]),
    ]
    for copy in raw_copies:
        copy.start()
    wcopies = [pltpu.make_async_copy(fw.at[l], wv.at[l], wsem.at[l]) for l in range(levels)]
    ncopy = pltpu.make_async_copy(nw, nwv, nwsem)
    first = [levels - 1] + list(range(LOC))
    for l in first:
        wcopies[l].start()
    ncopy.start()
    for l in range(LOC, levels - 1):
        wcopies[l].start()
    wready = set()

    def ready(l):
        if l not in wready:
            wcopies[l].wait()
            wready.add(l)

    wanted = [jnp.broadcast_to(order[q : q + 1, :], (16, BLK)) for q in range(nb)]
    step_iota = lax.broadcasted_iota(jnp.int32, (16, BLK), 0)

    def build(j, carry):
        base = pl.multiple_of(j * 16, 16)
        line = step_iota + base
        for q in range(nb):
            perm[pl.ds(base, 16), q * BLK : (q + 1) * BLK] = jnp.where(
                wanted[q] == line, 1.0, 0.0
            ).astype(BF)
        return carry

    lax.fori_loop(0, rows // 16, build, 0, unroll=4)

    def to_tree(d):
        stacked = jnp.concatenate(
            [raw[d, 0, 0], raw[d, 0, 1], raw[d, 1, 0], raw[d, 1, 1]], axis=0
        )
        for n in range(nb // 2):
            lo = n * 2 * BLK
            got = dot_nn(stacked, perm[:, lo : lo + 2 * BLK]).astype(BF)
            for e in range(2):
                xt[d, 2 * n + e] = got[:height, e * BLK : (e + 1) * BLK]
                vt[d, 2 * n + e] = got[height:, e * BLK : (e + 1) * BLK]

    def big(l, g):
        return jnp.concatenate(
            [wv[l, g, 0].reshape(2 * BLK, BLK), wv[l, g, 1].reshape(2 * BLK, BLK)], axis=1
        )

    def forward_level(l, cur, dst):
        ready(l)
        for g in range(nb):
            lhs = jnp.concatenate(
                [cur[pat[l, 0, g]], cur[pat[l, 1, g]]], axis=1
            )
            dst[g] = combine_forward(dot_nt(lhs, big(l, g)), cols).astype(BF)

    def masked_sum(pieces, spots, h):
        total = jnp.where(spots[0] == h, pieces[0], 0.0)
        for spot, piece in zip(spots[1:], pieces[1:]):
            total = total + jnp.where(spot == h, piece, 0.0)
        return total

    def adjoint_level(l, cur, dst):
        ready(l)
        for g in range(nb):
            out = dot_nn(conj_rows(cur[g], cols), big(l, g))
            contrib[2 * g] = out[:, :BLK]
            contrib[2 * g + 1] = out[:, BLK:]
        spots = [jnp.full((height, BLK), pat[l, j % 2, j // 2], jnp.int32) for j in range(2 * nb)]

        def sum_for(h):
            return masked_sum([contrib[j] for j in range(2 * nb)], spots, h)

        if l < LOC:

            def local(h, carry):
                dst[h] = sum_for(h).astype(BF)
                return carry

            lax.fori_loop(0, nb, local, 0)
            return None
        t = l - LOC

        def own(h, carry):
            aown[h] = sum_for(h)
            return carry

        def far(h, carry):
            asend[t, h] = sum_for(h + nb).astype(BF)
            return carry

        lax.fori_loop(0, nb, far, 0)
        copy = pltpu.make_async_remote_copy(
            src_ref=asend.at[t],
            dst_ref=arecv.at[t],
            send_sem=as_sem.at[t],
            recv_sem=ar_sem.at[t],
            device_id=partner_of(t),
            device_id_type=MESH,
        )
        copy.start()
        lax.fori_loop(0, nb, own, 0)
        return copy

    def adjoint_arrive(l, copy):
        copy.wait_recv()
        t = l - LOC
        for h in range(nb):
            bcur[l, h] = (aown[h] + arecv[t, h].astype(F32)).astype(BF)

    def forward_send(t):
        copy = pltpu.make_async_remote_copy(
            src_ref=fx[t].at[pl.ds(0, nb)],
            dst_ref=fx[t].at[pl.ds(nb, nb)],
            send_sem=fs_sem.at[t],
            recv_sem=fr_sem.at[t],
            device_id=partner_of(t),
            device_id_type=MESH,
        )
        return copy

    def near_parts(d):
        m0 = me_rhs * near
        for g in range(nb):
            acc = None
            for m in range(near):
                got = dot_nt(xt[d, nidx[m0 + m, g]], nwv[g, m].reshape(2 * BLK, BLK))
                got = combine_forward(got, cols)
                acc = got if acc is None else acc + got
            if d == 0:
                nf[g] = acc
            else:
                nsend[d - 1, 0, g] = acc.astype(BF)
        for h in range(nb):
            na[h] = jnp.zeros((height, BLK), F32) if d == 0 else na[h]
        for m in range(near):
            for g in range(nb):
                contrib[g] = dot_nn(
                    conj_rows(vt[d, g], cols), nwv[g, m].reshape(2 * BLK, BLK)
                )
            spots = [jnp.full((height, BLK), nidx[m0 + m, g], jnp.int32) for g in range(nb)]

            def one(h, carry):
                total = masked_sum([contrib[g] for g in range(nb)], spots, h)
                if d == 0:
                    na[h] = na[h] + total
                elif near == 1:
                    nsend[d - 1, 1, h] = total.astype(BF)
                else:
                    before = nsend[d - 1, 1, h].astype(F32) if m else 0.0
                    nsend[d - 1, 1, h] = (before + total).astype(BF)
                return carry

            lax.fori_loop(0, nb, one, 0)

    for copy in raw_copies:
        copy.wait()
    to_tree(0)
    pl.semaphore_wait(barrier, tops + n_rhs - 1)
    raw_sends = []
    for d in range(1, n_rhs):
        for which, ref in ((0, src), (1, prb)):
            copy = pltpu.make_async_remote_copy(
                src_ref=ref,
                dst_ref=raw.at[d, which],
                send_sem=xs_sem.at[d - 1, which],
                recv_sem=xr_sem.at[d - 1, which],
                device_id=peer(d),
                device_id_type=MESH,
            )
            copy.start()
            raw_sends.append(copy)
    sends_a = {}
    sends_f = {}
    sends_a[levels - 1] = adjoint_level(levels - 1, vt.at[0], None)
    cur = xt.at[0]
    for l in range(LOC):
        dst = fx[0].at[pl.ds(0, nb)] if l == LOC - 1 else fl.at[l]
        forward_level(l, cur, dst)
        cur = dst
    sends_f[0] = forward_send(0)
    sends_f[0].start()
    ncopy.wait()
    near_parts(0)
    near_sends = []
    for i in range(tops):
        sends_f[i].wait_recv()
        last = i == tops - 1
        forward_level(LOC + i, fx[i], ff if last else fx[i + 1].at[pl.ds(0, nb)])
        if not last:
            sends_f[i + 1] = forward_send(i + 1)
            sends_f[i + 1].start()
        if i == 0:
            for d in range(1, n_rhs):
                raw_sends[2 * (d - 1)].wait_recv()
                raw_sends[2 * (d - 1) + 1].wait_recv()
                to_tree(d)
                near_parts(d)
                copy = pltpu.make_async_remote_copy(
                    src_ref=nsend.at[d - 1],
                    dst_ref=nret.at[d - 1],
                    send_sem=ns_sem.at[d - 1],
                    recv_sem=nr_sem.at[d - 1],
                    device_id=origin(d),
                    device_id_type=MESH,
                )
                copy.start()
                near_sends.append(copy)
        if not last:
            la = levels - 1 - i
            adjoint_arrive(la, sends_a[la])
            sends_a[la - 1] = adjoint_level(la - 1, bcur.at[la], None)
        if i == tops - 2:
            adjoint_arrive(LOC, sends_a[LOC])
            for l in reversed(range(LOC)):
                adjoint_level(l, bcur.at[l + 1], bcur.at[l])

    for copy in near_sends:
        copy.wait_recv()
    lines_f, lines_a = [], []
    for g in range(nb):
        tf, ta = nf[g], na[g]
        for d in range(1, n_rhs):
            tf = tf + nret[d - 1, 0, g].astype(F32)
            ta = ta + nret[d - 1, 1, g].astype(F32)
        lines_f.append((ff[g].astype(F32) + tf).astype(BF))
        lines_a.append((bcur[0, g].astype(F32) + ta).astype(BF))
    tree = jnp.concatenate(
        [jnp.concatenate(lines_f, axis=1), jnp.concatenate(lines_a, axis=1)], axis=0
    )
    for n in range(nb // 2):
        lo = n * 2 * BLK
        got = dot_nt(tree, perm[lo : lo + 2 * BLK, :]).astype(BF)
        for z in range(2):
            out[0, z, :, lo : lo + 2 * BLK] = got[z * cols : (z + 1) * cols]
            out[1, z, :, lo : lo + 2 * BLK] = got[height + z * cols : height + (z + 1) * cols]

    for copy in raw_sends + near_sends + list(sends_f.values()) + list(sends_a.values()):
        copy.wait_send()


def body(n_rhs, sources, probe_field, factor_weight, factor_pattern, near_weight, near_index, tree_order):
    columns = sources.shape[1]
    rows = sources.shape[2]
    cols = -(-columns // 16) * 16
    if cols != columns:
        widen = ((0, 0), (0, cols - columns), (0, 0))
        sources = jnp.pad(sources, widen)
        probe_field = jnp.pad(probe_field, widen)
    nb = rows // BLK
    levels = factor_weight.shape[0]
    tops = levels - LOC
    near = near_weight.shape[1]
    height = 2 * cols
    block = (height, BLK)
    others = n_rhs - 1
    dma = pltpu.SemaphoreType.DMA
    any_spec = pl.BlockSpec(memory_space=pltpu.HBM)
    smem = pl.BlockSpec(memory_space=pltpu.SMEM)
    vmem = pl.BlockSpec(memory_space=pltpu.VMEM)
    out = jax.ShapeDtypeStruct((2, cols, rows), BF)
    both = pl.pallas_call(
        functools.partial(kernel, levels, nb, cols, near, n_rhs),
        out_shape=jax.ShapeDtypeStruct((2, 2, cols, rows), BF),
        in_specs=[any_spec, any_spec, any_spec, smem, any_spec, smem, vmem],
        out_specs=vmem,
        scratch_shapes=[
            pltpu.VMEM(factor_weight.shape, BF),
            pltpu.VMEM(near_weight.shape, BF),
            pltpu.VMEM((n_rhs, 2, 2, cols, rows), BF),
            pltpu.VMEM((rows, rows), BF),
            pltpu.VMEM((n_rhs, nb) + block, BF),
            pltpu.VMEM((n_rhs, nb) + block, BF),
            pltpu.VMEM((LOC, nb) + block, BF),
            [pltpu.VMEM((2 * nb,) + block, BF) for _ in range(tops)],
            pltpu.VMEM((nb,) + block, BF),
            pltpu.VMEM((levels, nb) + block, BF),
            pltpu.VMEM((2 * nb,) + block, F32),
            pltpu.VMEM((nb,) + block, F32),
            pltpu.VMEM((tops, nb) + block, BF),
            pltpu.VMEM((tops, nb) + block, BF),
            pltpu.VMEM((nb,) + block, F32),
            pltpu.VMEM((nb,) + block, F32),
            pltpu.VMEM((others, 2, nb) + block, BF),
            pltpu.VMEM((others, 2, nb) + block, BF),
            dma((levels,)),
            dma,
            dma((2,)),
            dma((others, 2)),
            dma((others, 2)),
            dma((tops,)),
            dma((tops,)),
            dma((tops,)),
            dma((tops,)),
            dma((others,)),
            dma((others,)),
        ],
        compiler_params=pltpu.CompilerParams(
            collective_id=0, has_side_effects=True, vmem_limit_bytes=60 * 2**20
        ),
    )(
        sources,
        probe_field,
        factor_weight,
        jnp.swapaxes(factor_pattern, 1, 2),
        near_weight,
        jnp.swapaxes(near_index, 0, 1),
        tree_order.reshape(nb, BLK),
    )
    forward_field, adjoint_field = both[0], both[1]
    return forward_field[:, :columns], adjoint_field[:, :columns]


def solution(mesh):
    rows = ("groups", "leaf", "half")
    return jax.shard_map(
        functools.partial(body, mesh.shape["rhs"]),
        mesh=mesh,
        in_specs=(
            P(None, "rhs", rows),
            P(None, "rhs", rows),
            P(None, rows, None, None, None, None),
            P(None, rows, None),
            P(rows, "rhs", None, None, None),
            P(rows, None),
            P(rows),
        ),
        out_specs=(P(None, "rhs", rows), P(None, "rhs", rows)),
        check_vma=False,
    )
```

```python
import functools

import jax
import jax.numpy as jnp
from jax import lax
from jax.experimental import pallas as pl
from jax.experimental.pallas import tpu as pltpu
from jax.sharding import PartitionSpec as P

BLK = 128
LOC = 3
BF = jnp.bfloat16
F32 = jnp.float32
MESH = pl.DeviceIdType.MESH


def flip(value, bit):
    return value + (1 - 2 * ((value // bit) % 2)) * bit


def partner_of(t):
    if t == 0:
        return {"half": flip(lax.axis_index("half"), 1)}
    return {"leaf": flip(lax.axis_index("leaf"), 2 ** (t - 1))}


def dot_nn(a, b):
    return lax.dot_general(a, b, (((1,), (0,)), ((), ())), preferred_element_type=F32)


def dot_nt(a, b):
    return lax.dot_general(a, b, (((1,), (1,)), ((), ())), preferred_element_type=F32)


def combine_forward(out, cols):
    real = out[:cols, :BLK] - out[cols:, BLK:]
    imag = out[cols:, :BLK] + out[:cols, BLK:]
    return jnp.concatenate([real, imag], axis=0)


def conj_rows(value, cols):
    real, imag = value[:cols], value[cols:]
    return jnp.concatenate(
        [jnp.concatenate([real, imag], axis=1), jnp.concatenate([imag, -real], axis=1)], axis=0
    )


def kernel(
    levels, nb, cols, near, n_rhs,
    src, prb, fw, pat_hbm, nw, nidx_hbm, order_hbm,
    out,
    pat, nidx, order, small_sem, wv, nwv, raw, perm, xt, vt, fl, fx, ff, bcur, contrib, aown, asend, arecv,
    nf, na, nsend, nret,
    wsem, nwsem, rawsem, xs_sem, xr_sem, fs_sem, fr_sem, as_sem, ar_sem, ns_sem, nr_sem,
):
    rows = nb * BLK
    height = 2 * cols
    tops = levels - LOC
    half = nb // 2
    me_rhs = lax.axis_index("rhs")

    def peer(d):
        return {"rhs": lax.rem(me_rhs + d, n_rhs)}

    def origin(d):
        return {"rhs": lax.rem(me_rhs + n_rhs - d, n_rhs)}

    barrier = pltpu.get_barrier_semaphore()
    for t in range(tops):
        pl.semaphore_signal(barrier, inc=1, device_id=partner_of(t), device_id_type=MESH)
    for d in range(1, n_rhs):
        pl.semaphore_signal(barrier, inc=1, device_id=peer(d), device_id_type=MESH)

    small_copies = [
        pltpu.make_async_copy(order_hbm, order, small_sem.at[0]),
        pltpu.make_async_copy(pat_hbm, pat, small_sem.at[1]),
        pltpu.make_async_copy(nidx_hbm, nidx, small_sem.at[2]),
    ]
    for copy in small_copies:
        copy.start()
    raw_copies = [
        pltpu.make_async_copy(src, raw.at[0, 0], rawsem.at[0]),
        pltpu.make_async_copy(prb, raw.at[0, 1], rawsem.at[1]),
    ]
    for copy in raw_copies:
        copy.start()
    wcopies = [pltpu.make_async_copy(fw.at[l], wv.at[l], wsem.at[l]) for l in range(levels)]
    ncopy = pltpu.make_async_copy(nw, nwv, nwsem)
    first = [levels - 1] + list(range(LOC))
    for l in first:
        wcopies[l].start()
    ncopy.start()
    for l in range(LOC, levels - 1):
        wcopies[l].start()
    wready = set()

    def ready(l):
        if l not in wready:
            wcopies[l].wait()
            wready.add(l)

    small_copies[0].wait()
    wanted = [jnp.broadcast_to(order[q : q + 1, :], (16, BLK)) for q in range(nb)]
    step_iota = lax.broadcasted_iota(jnp.int32, (16, BLK), 0)

    def build(j, carry):
        base = pl.multiple_of(j * 16, 16)
        line = step_iota + base
        for q in range(nb):
            perm[pl.ds(base, 16), q * BLK : (q + 1) * BLK] = jnp.where(
                wanted[q] == line, 1.0, 0.0
            ).astype(BF)
        return carry

    lax.fori_loop(0, rows // 16, build, 0, unroll=4)

    def to_tree(d):
        stacked = jnp.concatenate(
            [raw[d, 0, 0], raw[d, 0, 1], raw[d, 1, 0], raw[d, 1, 1]], axis=0
        )
        for n in range(nb // 2):
            lo = n * 2 * BLK
            got = dot_nn(stacked, perm[:, lo : lo + 2 * BLK]).astype(BF)
            for e in range(2):
                xt[d, 2 * n + e] = got[:height, e * BLK : (e + 1) * BLK]
                vt[d, 2 * n + e] = got[height:, e * BLK : (e + 1) * BLK]

    def big(l, g):
        return jnp.concatenate(
            [wv[l, g, 0].reshape(2 * BLK, BLK), wv[l, g, 1].reshape(2 * BLK, BLK)], axis=1
        )

    def forward_level(l, cur, dst, after=None):
        ready(l)
        for g in range(nb):
            lhs = jnp.concatenate(
                [cur[pat[l, 0, g]], cur[pat[l, 1, g]]], axis=1
            )
            dst[g] = combine_forward(dot_nt(lhs, big(l, g)), cols).astype(BF)
            if after is not None and (g + 1) % half == 0:
                after[g // half].start()

    def masked_sum(pieces, spots, h):
        total = jnp.where(spots[0] == h, pieces[0], 0.0)
        for spot, piece in zip(spots[1:], pieces[1:]):
            total = total + jnp.where(spot == h, piece, 0.0)
        return total

    def adjoint_level(l, cur, dst):
        ready(l)
        for g in range(nb):
            out = dot_nn(conj_rows(cur[g], cols), big(l, g))
            contrib[2 * g] = out[:, :BLK]
            contrib[2 * g + 1] = out[:, BLK:]
        spots = [jnp.full((height, BLK), pat[l, j % 2, j // 2], jnp.int32) for j in range(2 * nb)]

        def sum_for(h):
            return masked_sum([contrib[j] for j in range(2 * nb)], spots, h)

        if l < LOC:

            def local(h, carry):
                dst[h] = sum_for(h).astype(BF)
                return carry

            lax.fori_loop(0, nb, local, 0)
            return None
        t = l - LOC

        def own(h, carry):
            aown[h] = sum_for(h)
            return carry

        def far(h, carry):
            asend[t, h] = sum_for(h + nb).astype(BF)
            return carry

        copies = []
        for e in range(2):
            lax.fori_loop(e * half, (e + 1) * half, far, 0)
            part = pl.ds(e * half, half)
            copy = pltpu.make_async_remote_copy(
                src_ref=asend.at[t, part],
                dst_ref=arecv.at[t, part],
                send_sem=as_sem.at[t, e],
                recv_sem=ar_sem.at[t, e],
                device_id=partner_of(t),
                device_id_type=MESH,
            )
            copy.start()
            copies.append(copy)
        lax.fori_loop(0, nb, own, 0)
        return copies

    def adjoint_arrive(l, copies):
        t = l - LOC
        for h in range(nb):
            if h % half == 0:
                copies[h // half].wait_recv()
            bcur[l, h] = (aown[h] + arecv[t, h].astype(F32)).astype(BF)

    def forward_send(t):
        return [
            pltpu.make_async_remote_copy(
                src_ref=fx[t].at[pl.ds(e * half, half)],
                dst_ref=fx[t].at[pl.ds(nb + e * half, half)],
                send_sem=fs_sem.at[t, e],
                recv_sem=fr_sem.at[t, e],
                device_id=partner_of(t),
                device_id_type=MESH,
            )
            for e in range(2)
        ]

    def near_parts(d):
        m0 = me_rhs * near
        for g in range(nb):
            acc = None
            for m in range(near):
                got = dot_nt(xt[d, nidx[m0 + m, g]], nwv[g, m].reshape(2 * BLK, BLK))
                got = combine_forward(got, cols)
                acc = got if acc is None else acc + got
            if d == 0:
                nf[g] = acc
            else:
                nsend[d - 1, 0, g] = acc.astype(BF)
        for h in range(nb):
            na[h] = jnp.zeros((height, BLK), F32) if d == 0 else na[h]
        for m in range(near):
            for g in range(nb):
                contrib[g] = dot_nn(
                    conj_rows(vt[d, g], cols), nwv[g, m].reshape(2 * BLK, BLK)
                )
            spots = [jnp.full((height, BLK), nidx[m0 + m, g], jnp.int32) for g in range(nb)]

            def one(h, carry):
                total = masked_sum([contrib[g] for g in range(nb)], spots, h)
                if d == 0:
                    na[h] = na[h] + total
                elif near == 1:
                    nsend[d - 1, 1, h] = total.astype(BF)
                else:
                    before = nsend[d - 1, 1, h].astype(F32) if m else 0.0
                    nsend[d - 1, 1, h] = (before + total).astype(BF)
                return carry

            lax.fori_loop(0, nb, one, 0)

    for copy in raw_copies:
        copy.wait()
    to_tree(0)
    pl.semaphore_wait(barrier, tops + n_rhs - 1)
    raw_sends = []
    for d in range(1, n_rhs):
        for which, ref in ((0, src), (1, prb)):
            copy = pltpu.make_async_remote_copy(
                src_ref=ref,
                dst_ref=raw.at[d, which],
                send_sem=xs_sem.at[d - 1, which],
                recv_sem=xr_sem.at[d - 1, which],
                device_id=peer(d),
                device_id_type=MESH,
            )
            copy.start()
            raw_sends.append(copy)
    small_copies[1].wait()
    small_copies[2].wait()
    sends_a = {}
    sends_f = {}
    sends_a[levels - 1] = adjoint_level(levels - 1, vt.at[0], None)
    cur = xt.at[0]
    for l in range(LOC):
        dst = fx[0].at[pl.ds(0, nb)] if l == LOC - 1 else fl.at[l]
        if l == LOC - 1:
            sends_f[0] = forward_send(0)
        forward_level(l, cur, dst, sends_f.get(0))
        cur = dst
    near_sends = []
    for i in range(tops):
        for copy in sends_f[i]:
            copy.wait_recv()
        last = i == tops - 1
        if not last:
            sends_f[i + 1] = forward_send(i + 1)
        forward_level(LOC + i, fx[i], ff if last else fx[i + 1].at[pl.ds(0, nb)], sends_f.get(i + 1))
        if i == 0:
            ncopy.wait()
            near_parts(0)
            for d in range(1, n_rhs):
                raw_sends[2 * (d - 1)].wait_recv()
                raw_sends[2 * (d - 1) + 1].wait_recv()
                to_tree(d)
                near_parts(d)
                copy = pltpu.make_async_remote_copy(
                    src_ref=nsend.at[d - 1],
                    dst_ref=nret.at[d - 1],
                    send_sem=ns_sem.at[d - 1],
                    recv_sem=nr_sem.at[d - 1],
                    device_id=origin(d),
                    device_id_type=MESH,
                )
                copy.start()
                near_sends.append(copy)
        if not last:
            la = levels - 1 - i
            adjoint_arrive(la, sends_a[la])
            sends_a[la - 1] = adjoint_level(la - 1, bcur.at[la], None)
        if i == tops - 2:
            adjoint_arrive(LOC, sends_a[LOC])
            for l in reversed(range(LOC)):
                adjoint_level(l, bcur.at[l + 1], bcur.at[l])

    for copy in near_sends:
        copy.wait_recv()
    lines_f, lines_a = [], []
    for g in range(nb):
        tf, ta = nf[g], na[g]
        for d in range(1, n_rhs):
            tf = tf + nret[d - 1, 0, g].astype(F32)
            ta = ta + nret[d - 1, 1, g].astype(F32)
        lines_f.append((ff[g].astype(F32) + tf).astype(BF))
        lines_a.append((bcur[0, g].astype(F32) + ta).astype(BF))
    tree = jnp.concatenate(
        [jnp.concatenate(lines_f, axis=1), jnp.concatenate(lines_a, axis=1)], axis=0
    )
    for n in range(nb // 2):
        lo = n * 2 * BLK
        got = dot_nt(tree, perm[lo : lo + 2 * BLK, :]).astype(BF)
        for z in range(2):
            out[0, z, :, lo : lo + 2 * BLK] = got[z * cols : (z + 1) * cols]
            out[1, z, :, lo : lo + 2 * BLK] = got[height + z * cols : height + (z + 1) * cols]

    level_sends = [c for pair in list(sends_f.values()) + list(sends_a.values()) for c in pair]
    for copy in raw_sends + near_sends + level_sends:
        copy.wait_send()


def body(n_rhs, sources, probe_field, factor_weight, factor_pattern, near_weight, near_index, tree_order):
    columns = sources.shape[1]
    rows = sources.shape[2]
    cols = -(-columns // 16) * 16
    if cols != columns:
        widen = ((0, 0), (0, cols - columns), (0, 0))
        sources = jnp.pad(sources, widen)
        probe_field = jnp.pad(probe_field, widen)
    nb = rows // BLK
    levels = factor_weight.shape[0]
    tops = levels - LOC
    near = near_weight.shape[1]
    height = 2 * cols
    block = (height, BLK)
    others = n_rhs - 1
    dma = pltpu.SemaphoreType.DMA
    any_spec = pl.BlockSpec(memory_space=pltpu.HBM)
    vmem = pl.BlockSpec(memory_space=pltpu.VMEM)
    out = jax.ShapeDtypeStruct((2, cols, rows), BF)
    both = pl.pallas_call(
        functools.partial(kernel, levels, nb, cols, near, n_rhs),
        out_shape=jax.ShapeDtypeStruct((2, 2, cols, rows), BF),
        in_specs=[any_spec] * 7,
        out_specs=vmem,
        scratch_shapes=[
            pltpu.SMEM((levels, 2, nb), jnp.int32),
            pltpu.SMEM((near_index.shape[1], nb), jnp.int32),
            pltpu.VMEM((nb, BLK), jnp.int32),
            dma((3,)),
            pltpu.VMEM(factor_weight.shape, BF),
            pltpu.VMEM(near_weight.shape, BF),
            pltpu.VMEM((n_rhs, 2, 2, cols, rows), BF),
            pltpu.VMEM((rows, rows), BF),
            pltpu.VMEM((n_rhs, nb) + block, BF),
            pltpu.VMEM((n_rhs, nb) + block, BF),
            pltpu.VMEM((LOC, nb) + block, BF),
            [pltpu.VMEM((2 * nb,) + block, BF) for _ in range(tops)],
            pltpu.VMEM((nb,) + block, BF),
            pltpu.VMEM((levels, nb) + block, BF),
            pltpu.VMEM((2 * nb,) + block, F32),
            pltpu.VMEM((nb,) + block, F32),
            pltpu.VMEM((tops, nb) + block, BF),
            pltpu.VMEM((tops, nb) + block, BF),
            pltpu.VMEM((nb,) + block, F32),
            pltpu.VMEM((nb,) + block, F32),
            pltpu.VMEM((others, 2, nb) + block, BF),
            pltpu.VMEM((others, 2, nb) + block, BF),
            dma((levels,)),
            dma,
            dma((2,)),
            dma((others, 2)),
            dma((others, 2)),
            dma((tops, 2)),
            dma((tops, 2)),
            dma((tops, 2)),
            dma((tops, 2)),
            dma((others,)),
            dma((others,)),
        ],
        compiler_params=pltpu.CompilerParams(
            collective_id=0, has_side_effects=True, vmem_limit_bytes=60 * 2**20
        ),
    )(
        sources,
        probe_field,
        factor_weight,
        jnp.swapaxes(factor_pattern, 1, 2),
        near_weight,
        jnp.swapaxes(near_index, 0, 1),
        tree_order.reshape(nb, BLK),
    )
    forward_field, adjoint_field = both[0], both[1]
    return forward_field[:, :columns], adjoint_field[:, :columns]


def solution(mesh):
    rows = ("groups", "leaf", "half")
    return jax.shard_map(
        functools.partial(body, mesh.shape["rhs"]),
        mesh=mesh,
        in_specs=(
            P(None, "rhs", rows),
            P(None, "rhs", rows),
            P(None, rows, None, None, None, None),
            P(None, rows, None),
            P(rows, "rhs", None, None, None),
            P(rows, None),
            P(rows),
        ),
        out_specs=(P(None, "rhs", rows), P(None, "rhs", rows)),
        check_vma=False,
    )
```
